32 devices in a mesh: groups: 2 (over y), dom: 4 (over z), sub: 2 (over x), comp: 2 (over core).
Axes of the slice: x: 2, y: 2, z: 4, core: 2. Of those that a mesh axis runs over, the one named last changes fastest.
Arguments:
- displacement: float32 [3, 262144], P(None, ('groups', 'dom', 'sub', 'comp')), parts along dimension 1, may hold values from -6 to 6
- far_lists: int32 [128, 64], P(('groups', 'dom', 'sub', 'comp')), parts along dimension 0, may hold values from 0 to 8191, as said below
- far_counts: int32 [128], P(('groups', 'dom', 'sub', 'comp')), parts along dimension 0, may hold values from 0 to 64, as said below
- near_lists: int32 [128, 128], P(('groups', 'dom', 'sub', 'comp')), parts along dimension 0, may hold values from 0 to 8447, as said below
- near_counts: int32 [128], P(('groups', 'dom', 'sub', 'comp')), parts along dimension 0, may hold values from 1 to 128, as said below
- connectivity: int32 [125, 4096], P(None, ('groups', 'dom', 'sub', 'comp')), parts along dimension 1, may hold values from 0 to 8703, as said below
- inverse_jacobian: float32 [9, 4096], P(None, ('groups', 'dom', 'sub', 'comp')), parts along dimension 1, may hold values from -2 to 2
- lame_first: bfloat16 [125, 4096], P(None, ('groups', 'dom', 'sub', 'comp')), parts along dimension 1, may hold values from 0.0039978027 to 0.039794922
- lame_shear: bfloat16 [125, 4096], P(None, ('groups', 'dom', 'sub', 'comp')), parts along dimension 1, may hold values from 0.0039978027 to 0.039794922
Outputs:
- assembled: float32 [3, 262144], P(None, ('groups', 'dom', 'sub', 'comp')), parts along dimension 1
The draws below stay inside these ranges and needn't reach their ends.
There are 2 independent parts, one for each index of `groups`. The reference program is written for one: setup_inputs(seed, part) draws one part's arguments, and reference() takes and returns one part's arrays. A program takes and returns all parts, laid end to end along the dimension named above; each array names one. Nothing has to cross between parts.
Inputs may be any that keep to these rules, and one draw needn't show every extreme that they name: far_counts of a device towards its own partition is 0 and towards every other partition 1 or more; some count reaches 64. Used entries of one far list are distinct owned nodes. `far_lists`: entries are owned node numbers of the sending device. `near_counts`: every near count is 1 or more, some reaches 128. `near_lists`: each used entry names an owned node or a used slot of the device's far_recv. `connectivity`: the first 64 elements of every device name only owned nodes (below 8192); the others name owned nodes or used ghost slots; an element may name a position more than once.
All inputs are finite; a program needn't handle non-finite values.
Results may differ from the reference program's by a relative error of at most 0.0003.
Values sent between devices are 32-bit elements; how exact they have to be, the bound alone decides.
A program may use at most 64 MiB of HBM per device.

```python
import math
from functools import partial
import jax
import jax.numpy as jnp
import numpy as np
from jax import lax

POINTS = 125
E_DEV = 128
E_INNER = 64
NODE_DEV = 8192
CAP_FAR = 64
CAP_NEAR = 128
PEERS = 4
SHARDS = 16
NODES = 131072
ELEMS = 2048
STACK = 8448
LOCAL = 8704
N_DOM = 4


def routing(key):
    subkeys = jax.random.split(key, 16)
    dom_of = jnp.arange(SHARDS, dtype=jnp.int32) // PEERS
    peer_of = jnp.arange(SHARDS, dtype=jnp.int32) % PEERS
    heavy_far = jax.random.randint(subkeys[0], (SHARDS, 1), 0, 2)
    light_load = jax.random.randint(subkeys[1], (SHARDS, N_DOM), 1, CAP_FAR // 4 + 1)
    heavy_load = jax.random.randint(subkeys[2], (SHARDS, N_DOM), CAP_FAR // 2, CAP_FAR + 1)
    far_counts = jnp.where(heavy_far == 1, heavy_load, light_load)
    far_counts = jnp.where(dom_of[:, None] == jnp.arange(N_DOM)[None, :], 0, far_counts)
    far_counts = far_counts.at[0, 1].set(CAP_FAR)
    far_counts = far_counts.at[(N_DOM - 1) * PEERS, 0].set(CAP_FAR)
    far_base = jax.random.randint(subkeys[3], (SHARDS, N_DOM, 1), 0, NODE_DEV)
    far_base = far_base.at[0, 1, 0].set(NODE_DEV - 1)
    far_stride = 2 * jax.random.randint(subkeys[4], (SHARDS, N_DOM, 1), 0, NODE_DEV // 2) + 1
    far_lists = (far_base + jnp.arange(CAP_FAR, dtype=jnp.int32)[None, None, :] * far_stride) % NODE_DEV
    heavy_near = jax.random.randint(subkeys[5], (SHARDS, 1), 0, 2)
    light_near = jax.random.randint(subkeys[6], (SHARDS, PEERS), 1, CAP_NEAR // 4 + 1)
    heavy_near_load = jax.random.randint(subkeys[7], (SHARDS, PEERS), CAP_NEAR // 2, CAP_NEAR + 1)
    near_counts = jnp.where(heavy_near == 1, heavy_near_load, light_near)
    near_counts = near_counts.at[0, 1].set(CAP_NEAR)
    near_counts = near_counts.at[PEERS - 1, 0].set(CAP_NEAR)
    shape_near = (SHARDS, PEERS, CAP_NEAR)
    pick_far = jax.random.randint(subkeys[8], shape_near, 0, 2)
    owned_pick = jax.random.randint(subkeys[9], shape_near, 0, NODE_DEV)
    offset = jax.random.randint(subkeys[10], shape_near, 1, N_DOM)
    source_dom = (dom_of[:, None, None] + offset) % N_DOM
    source_dev = source_dom * PEERS + peer_of[:, None, None]
    source_count = far_counts[source_dev, jnp.broadcast_to(dom_of[:, None, None], shape_near)]
    slot_pick = jax.random.randint(subkeys[11], shape_near, 0, CAP_FAR) % jnp.maximum(source_count, 1)
    far_position = NODE_DEV + source_dom * CAP_FAR + slot_pick
    near_lists = jnp.where(pick_far == 1, far_position, owned_pick)
    near_lists = near_lists.at[0, 0, 0].set(NODE_DEV + N_DOM * CAP_FAR - 1)
    shape_conn = (POINTS, SHARDS, E_DEV)
    pick_ghost = jax.random.randint(subkeys[12], shape_conn, 0, 2)
    pick_ghost = jnp.where(jnp.arange(E_DEV)[None, None, :] >= E_INNER, pick_ghost, 0)
    owned_node = jax.random.randint(subkeys[13], shape_conn, 0, NODE_DEV)
    target_peer = jax.random.randint(subkeys[14], shape_conn, 0, PEERS)
    sender_dev = dom_of[None, :, None] * PEERS + target_peer
    sender_count = near_counts[sender_dev, jnp.broadcast_to(peer_of[None, :, None], shape_conn)]
    ghost_slot = jax.random.randint(subkeys[15], shape_conn, 0, CAP_NEAR) % sender_count
    ghost_position = NODE_DEV + target_peer * CAP_NEAR + ghost_slot
    connectivity = jnp.where(pick_ghost == 1, ghost_position, owned_node)
    connectivity = connectivity.at[0, 0, E_DEV - 1].set(NODE_DEV + PEERS * CAP_NEAR - 1)
    return (far_lists.reshape(SHARDS * N_DOM, CAP_FAR).astype(jnp.int32), far_counts.reshape(SHARDS * N_DOM).astype(jnp.int32), near_lists.reshape(SHARDS * PEERS, CAP_NEAR).astype(jnp.int32), near_counts.reshape(SHARDS * PEERS).astype(jnp.int32), connectivity.reshape(POINTS, SHARDS * E_DEV).astype(jnp.int32))


def draw_far_lists(key, part):
    drawn = routing(key)
    return drawn[0]


def draw_far_counts(key, part):
    drawn = routing(key)
    return drawn[1]


def draw_near_lists(key, part):
    drawn = routing(key)
    return drawn[2]


def draw_near_counts(key, part):
    drawn = routing(key)
    return drawn[3]


def draw_connectivity(key, part):
    drawn = routing(key)
    return drawn[4]


def block_levels(stream_key, dims, cuts, low, largest):
    def one(axis_at, parts):
        steps = jax.random.uniform(jax.random.fold_in(jax.random.fold_in(stream_key, 6), axis_at), (parts,), jnp.float32, low / len(cuts), largest / len(cuts))
        return jnp.repeat(jnp.exp(steps), dims[axis_at] // parts).reshape((-1,) + (1,) * (len(dims) - axis_at - 1))

    level = one(*cuts[0])
    for cut in cuts[1:]:
        level = level * one(*cut)
    return level


def gaussian(key, shape, width, most, cuts=(), kind=jnp.bfloat16):
    values = width * jax.random.normal(key, shape, jnp.float32)
    if cuts:
        values = values * block_levels(key, shape, cuts, -0.22, 0.18)
    return jnp.clip(values, -most, most).astype(kind)


def setup_inputs(seed: int = 0, part: int = 0) -> dict:
    key_of = jax.random.split(jax.random.key(seed), 10)
    part_keys = jax.random.split(jax.random.fold_in(key_of[9], part), 10)
    return {
        "displacement": gaussian(part_keys[0], (3, NODES), 1.0, 6.0, ((1, 16),), jnp.float32),
        "far_lists": draw_far_lists(jax.random.fold_in(jax.random.fold_in(key_of[9], part), 71), part),
        "far_counts": draw_far_counts(jax.random.fold_in(jax.random.fold_in(key_of[9], part), 71), part),
        "near_lists": draw_near_lists(jax.random.fold_in(jax.random.fold_in(key_of[9], part), 71), part),
        "near_counts": draw_near_counts(jax.random.fold_in(jax.random.fold_in(key_of[9], part), 71), part),
        "connectivity": draw_connectivity(jax.random.fold_in(jax.random.fold_in(key_of[9], part), 71), part),
        "inverse_jacobian": gaussian(part_keys[6], (9, ELEMS), 0.3, 2.0, ((1, 16),), jnp.float32),
        "lame_first": jnp.clip(jnp.exp(math.log(0.039794922) - 2.2979944 * jax.random.uniform(part_keys[7], (POINTS, ELEMS), jnp.float32) ** block_levels(part_keys[7], (POINTS, ELEMS), ((1, 16),), -0.2, 0.2)), 0.0039978027, 0.039794922).astype(jnp.bfloat16),
        "lame_shear": jnp.clip(jnp.exp(math.log(0.039794922) - 2.2979944 * jax.random.uniform(part_keys[8], (POINTS, ELEMS), jnp.float32) ** block_levels(part_keys[8], (POINTS, ELEMS), ((1, 16),), -0.2, 0.2)), 0.0039978027, 0.039794922).astype(jnp.bfloat16),
    }


def basis_tables():
    gll_points = np.array([-1.0, -math.sqrt(3.0 / 7.0), 0.0, math.sqrt(3.0 / 7.0), 1.0])
    inner_root = math.sqrt(5.0 - 2.0 * math.sqrt(10.0 / 7.0)) / 3.0
    outer_root = math.sqrt(5.0 + 2.0 * math.sqrt(10.0 / 7.0)) / 3.0
    gauss_points = np.array([-outer_root, -inner_root, 0.0, inner_root, outer_root])
    values = np.zeros((5, 5))
    slopes = np.zeros((5, 5))
    for q in range(5):
        for n in range(5):
            product = 1.0
            for m in range(5):
                if m != n:
                    product = product * (gauss_points[q] - gll_points[m]) / (gll_points[n] - gll_points[m])
            values[q, n] = product
            total = 0.0
            for l in range(5):
                if l != n:
                    term = 1.0 / (gll_points[n] - gll_points[l])
                    for m in range(5):
                        if m != n and m != l:
                            term = term * (gauss_points[q] - gll_points[m]) / (gll_points[n] - gll_points[m])
                    total = total + term
            slopes[q, n] = total
    return (values, slopes)

def dense_tables():
    values, slopes = basis_tables()
    stacked_tables = []
    for r in range(3):
        factors = [slopes if d == r else values for d in range(3)]
        stacked_tables.append(np.kron(np.kron(factors[0], factors[1]), factors[2]))
    return jnp.asarray(np.stack(stacked_tables), jnp.float32)

def material(gref, jacobian, first_lame, shear_lame):
    gradient = lax.optimization_barrier(jnp.sum(jacobian[None, :, :, None, :] * gref[:, :, None, :, :], axis=1))
    strain = 0.5 * (gradient + jnp.swapaxes(gradient, 0, 1))
    trace_sum = gradient[0, 0] + gradient[1, 1] + gradient[2, 2]
    identity = jnp.eye(3, dtype=jnp.float32)[:, :, None, None]
    stress = 2.0 * shear_lame * strain + first_lame * trace_sum * identity
    return lax.optimization_barrier(jnp.sum(jacobian[None, :, :, None, :] * stress[:, None, :, :, :], axis=2))

def shard_terms(operands):
    local_values, links, jacobian9, first_raw, shear_raw = operands
    tables = dense_tables()
    elements = links.shape[1]
    nodal = local_values[:, links]
    jacobian = jacobian9.reshape(3, 3, elements)
    gref = jnp.einsum('rqn,cne->crqe', tables, nodal, precision=lax.Precision.HIGHEST)
    tref = material(gref, jacobian, first_raw.astype(jnp.float32), shear_raw.astype(jnp.float32))
    element_out = jnp.einsum('rqn,crqe->cne', tables, tref, precision=lax.Precision.HIGHEST)
    return jnp.zeros((3, LOCAL), jnp.float32).at[:, links].add(element_out)

def add_into(positions, contributions, extent):
    return jnp.zeros((3, extent), jnp.float32).at[:, positions].add(contributions)

def reference(displacement, far_lists, far_counts, near_lists, near_counts, connectivity, inverse_jacobian, lame_first, lame_shear):
    owned_all = displacement.reshape(3, SHARDS, NODE_DEV)
    far_index = far_lists.reshape(SHARDS, N_DOM * CAP_FAR)
    far_mask = (jnp.arange(CAP_FAR)[None, None, :] < far_counts.reshape(SHARDS, N_DOM)[:, :, None]).reshape(SHARDS, N_DOM * CAP_FAR)
    far_mask = far_mask.astype(jnp.float32)
    sent_far = jnp.take_along_axis(owned_all, far_index[None], axis=2) * far_mask[None]
    far_recv = sent_far.reshape(3, N_DOM, PEERS, N_DOM, CAP_FAR).transpose(0, 3, 2, 1, 4).reshape(3, SHARDS, N_DOM * CAP_FAR)
    stacked = jnp.concatenate([owned_all, far_recv], axis=2)
    near_index = near_lists.reshape(SHARDS, PEERS * CAP_NEAR)
    near_mask = (jnp.arange(CAP_NEAR)[None, None, :] < near_counts.reshape(SHARDS, PEERS)[:, :, None]).reshape(SHARDS, PEERS * CAP_NEAR)
    near_mask = near_mask.astype(jnp.float32)
    sent_near = jnp.take_along_axis(stacked, near_index[None], axis=2) * near_mask[None]
    near_recv = sent_near.reshape(3, N_DOM, PEERS, PEERS, CAP_NEAR).transpose(0, 1, 3, 2, 4).reshape(3, SHARDS, PEERS * CAP_NEAR)
    local_values = jnp.concatenate([owned_all, near_recv], axis=2)
    operands = (local_values.transpose(1, 0, 2), connectivity.reshape(POINTS, SHARDS, E_DEV).transpose(1, 0, 2), inverse_jacobian.reshape(9, SHARDS, E_DEV).transpose(1, 0, 2), lame_first.reshape(POINTS, SHARDS, E_DEV).transpose(1, 0, 2), lame_shear.reshape(POINTS, SHARDS, E_DEV).transpose(1, 0, 2))
    local_sum = lax.map(shard_terms, operands).transpose(1, 0, 2)
    owned_sum = local_sum[:, :, :NODE_DEV]
    ghost_sum = local_sum[:, :, NODE_DEV:].reshape(3, N_DOM, PEERS, PEERS, CAP_NEAR).transpose(0, 1, 3, 2, 4).reshape(3, SHARDS, PEERS * CAP_NEAR)
    ghost_sum = ghost_sum * near_mask[None]
    stack_sum = jax.vmap(partial(add_into, extent=STACK), in_axes=(0, 1), out_axes=1)(near_index, ghost_sum)
    stack_sum = stack_sum.at[:, :, :NODE_DEV].add(owned_sum)
    far_back = stack_sum[:, :, NODE_DEV:].reshape(3, N_DOM, PEERS, N_DOM, CAP_FAR).transpose(0, 3, 2, 1, 4).reshape(3, SHARDS, N_DOM * CAP_FAR)
    far_back = far_back * far_mask[None]
    owner_sum = jax.vmap(partial(add_into, extent=NODE_DEV), in_axes=(0, 1), out_axes=1)(far_index, far_back)
    assembled = stack_sum[:, :, :NODE_DEV] + owner_sum
    return assembled.reshape(3, NODES)
```

```python
import functools
import math

import jax
import jax.numpy as jnp
import numpy as np
from jax import lax
from jax.experimental import pallas as pl
from jax.experimental.pallas import tpu as pltpu
from jax.sharding import PartitionSpec as P

F32 = jnp.float32
BF16 = jnp.bfloat16
LANES = 128
ROWS = 64
NOWHERE = 16383
HIGH = 48
MESH = pl.DeviceIdType.MESH


def basis_tables():
    gll_points = np.array([-1.0, -math.sqrt(3.0 / 7.0), 0.0, math.sqrt(3.0 / 7.0), 1.0])
    inner_root = math.sqrt(5.0 - 2.0 * math.sqrt(10.0 / 7.0)) / 3.0
    outer_root = math.sqrt(5.0 + 2.0 * math.sqrt(10.0 / 7.0)) / 3.0
    gauss_points = np.array([-outer_root, -inner_root, 0.0, inner_root, outer_root])
    values = np.zeros((5, 5))
    slopes = np.zeros((5, 5))
    for q in range(5):
        for n in range(5):
            product = 1.0
            for m in range(5):
                if m != n:
                    product = (
                        product
                        * (gauss_points[q] - gll_points[m])
                        / (gll_points[n] - gll_points[m])
                    )
            values[q, n] = product
            total = 0.0
            for l in range(5):
                if l != n:
                    term = 1.0 / (gll_points[n] - gll_points[l])
                    for m in range(5):
                        if m != n and m != l:
                            term = (
                                term
                                * (gauss_points[q] - gll_points[m])
                                / (gll_points[n] - gll_points[m])
                            )
                    total = total + term
            slopes[q, n] = total
    return (values, slopes)


def split_tables():
    values, slopes = basis_tables()
    forward = np.zeros((3, LANES, LANES), np.float32)
    for r in range(3):
        factors = [slopes if d == r else values for d in range(3)]
        forward[r, :125, :125] = np.kron(np.kron(factors[0], factors[1]), factors[2])
    stacked = forward.reshape(3 * LANES, LANES)
    top = stacked.astype(jnp.bfloat16)
    rest = (stacked - top.astype(np.float32)).astype(jnp.bfloat16)
    fwd = np.concatenate([top, rest, top], axis=1)
    bwd = np.concatenate([top.T, rest.T, top.T], axis=1)
    return np.ascontiguousarray(fwd), np.ascontiguousarray(bwd)


def split(x):
    top = x.astype(BF16)
    return top, (x - top.astype(F32)).astype(BF16)


def onehot(rows, key):
    grid = lax.broadcasted_iota(jnp.int32, (rows, key.shape[1]), 0)
    return jnp.where(grid == key, 1.0, 0.0).astype(BF16)


def pick(table, rows):
    found = [[], [], []]
    for at in range(0, len(rows), 2):
        pair = jnp.concatenate(rows[at : at + 2], axis=1)
        high = onehot(LANES, pair >> 7)
        dense = jnp.dot(
            table, jnp.concatenate([high, high], axis=0), preferred_element_type=F32
        )
        low = lax.broadcasted_iota(jnp.int32, (LANES, 2 * LANES), 0) == (pair & 127)
        for c in range(3):
            part = dense[c * LANES : (c + 1) * LANES]
            line = jnp.sum(jnp.where(low, part, 0.0), axis=0, keepdims=True)
            found[c] += [line[:, :LANES], line[:, LANES:]]
    return found


def spread(rows, values):
    key = jnp.concatenate(rows, axis=1)
    low = onehot(2 * LANES, key & 255)
    high = onehot(HIGH, key >> 8)
    parts = []
    for c in range(3):
        top, rest = split(jnp.concatenate(values[c], axis=1))
        parts += [high * top, high * rest]
    return lax.dot_general(
        jnp.concatenate(parts, axis=0),
        low,
        (((1,), (1,)), ((), ())),
        preferred_element_type=F32,
    )


def joined(acc, c):
    return acc[2 * HIGH * c : 2 * HIGH * c + HIGH] + acc[2 * HIGH * c + HIGH : 2 * HIGH * (c + 1)]


def kernel(
    n_dom,
    n_sub,
    n_comp,
    far_counts,
    near_counts,
    disp,
    far_lists,
    near_lists,
    conn,
    jac,
    lame_first,
    lame_shear,
    fwd,
    bwd,
    out,
    tab,
    table,
    far_index,
    index,
    nodal,
    first,
    shear,
    acc_in,
    acc_out,
    far_out,
    far_in,
    near_out,
    near_in,
    ghost_out,
    ghost_in,
    back_out,
    back_in,
    send_far,
    recv_far,
    send_near,
    recv_near,
    send_ghost,
    recv_ghost,
    send_back,
    recv_back,
):
    n_peers = n_sub * n_comp
    owned = disp.shape[1] // LANES
    dom = lax.axis_index("dom")
    peer = lax.axis_index("sub") * n_comp + lax.axis_index("comp")

    def dom_id(step):
        return {"dom": lax.rem(dom + step, n_dom)}

    def peer_id(step):
        other = lax.rem(peer + step, n_peers)
        return {"sub": other // n_comp, "comp": lax.rem(other, n_comp)}

    def far_copies(source, target, send, recv):
        return [
            pltpu.make_async_remote_copy(
                src_ref=source.at[lax.rem(dom + step, n_dom)],
                dst_ref=target.at[dom],
                send_sem=send.at[step],
                recv_sem=recv.at[step],
                device_id=dom_id(step),
                device_id_type=MESH,
            )
            for step in range(1, n_dom)
        ]

    def near_copies(source, target, send, recv):
        return [
            pltpu.make_async_remote_copy(
                src_ref=source.at[lax.rem(peer + step, n_peers)],
                dst_ref=target.at[peer],
                send_sem=send.at[step],
                recv_sem=recv.at[step],
                device_id=peer_id(step),
                device_id_type=MESH,
            )
            for step in range(1, n_peers)
        ]

    barrier = pltpu.get_barrier_semaphore()
    for step in range(1, n_dom):
        pl.semaphore_signal(barrier, inc=1, device_id=dom_id(step), device_id_type=MESH)
    for step in range(1, n_peers):
        pl.semaphore_signal(barrier, inc=1, device_id=peer_id(step), device_id_type=MESH)

    lane8 = lax.broadcasted_iota(jnp.int32, (8, LANES), 1)
    lane = lax.broadcasted_iota(jnp.int32, (1, LANES), 1)

    for c in range(3):
        tab[c, owned:, :] = jnp.zeros((LANES - owned, LANES), F32)
        for h in range(owned):
            tab[c, h : h + 1, :] = disp[c : c + 1, h * LANES : (h + 1) * LANES]

    def turn():
        for c in range(3):
            top, rest = split(tab[c].T)
            table[c * LANES : (c + 1) * LANES, :LANES] = top
            table[c * LANES : (c + 1) * LANES, LANES:] = rest

    turn()

    far_index[...] = jnp.zeros_like(far_index)
    far_index[:n_dom, :64] = far_lists[...]
    listed = far_index[...]
    lane_f = lax.broadcasted_iota(jnp.int32, listed.shape, 1)
    listed = jnp.where(lane_f < 64, listed, pltpu.roll(listed, 64, 1))
    far_rows = [
        jnp.where((lane & 63) < far_counts[p], listed[p : p + 1], NOWHERE) for p in range(n_dom)
    ]
    near_rows = [
        jnp.where(lane < near_counts[t], near_lists[t : t + 1, :], NOWHERE)
        for t in range(n_peers)
    ]

    far_out[...] = jnp.zeros_like(far_out)
    near_out[...] = jnp.zeros_like(near_out)
    ghost_out[...] = jnp.zeros_like(ghost_out)
    back_out[...] = jnp.zeros_like(back_out)

    found = pick(table[...], far_rows)
    for p in range(n_dom):
        for c in range(3):
            far_out[p, c : c + 1, :] = found[c][p]
    far_in[dom] = jnp.zeros((8, LANES), F32)
    back_in[dom] = jnp.zeros((8, LANES), F32)

    pl.semaphore_wait(barrier, n_dom - 1 + n_peers - 1)
    sends = far_copies(far_out, far_in, send_far, recv_far)
    for copy in sends:
        copy.start()

    tab_rows = jnp.full((8, LANES), NOWHERE, jnp.int32)
    index[0, 120:128, :] = tab_rows
    index[0, :125, :] = conn[...]
    low_half = index[0, :ROWS, :]
    high_half = index[0, ROWS:, :]
    lane64 = lax.broadcasted_iota(jnp.int32, (ROWS, LANES), 1)
    packed_in = jnp.where(lane64 < 64, low_half, pltpu.roll(high_half, 64, 1))
    packed_out = jnp.where(lane64 < 64, pltpu.roll(low_half, 64, 1), high_half)
    index[1, :ROWS, :] = packed_in
    index[1, ROWS:, :] = packed_out

    first[120:128, :] = jnp.zeros((8, LANES), F32)
    shear[120:128, :] = jnp.zeros((8, LANES), F32)
    first[:125, :] = lame_first[...].astype(F32)
    shear[:125, :] = lame_shear[...].astype(F32)

    def gather(half):
        def body(step, _):
            at = pl.multiple_of(half * ROWS + step * 8, 8)
            block = index[1, pl.ds(at, 8), :]
            got = pick(table[...], [block[r : r + 1] for r in range(8)])
            for c in range(3):
                nodal[c, pl.ds(at, 8), :] = jnp.concatenate(got[c], axis=0)
            return 0

        lax.fori_loop(0, ROWS // 8, body, 0)

    def scatter(half, acc):
        acc[...] = jnp.zeros_like(acc)

        def body(step, _):
            at = pl.multiple_of(half * ROWS + step * 8, 8)
            block = index[1, pl.ds(at, 8), :]
            terms = [nodal[c, pl.ds(at, 8), :] for c in range(3)]
            acc[...] += spread(
                [block[r : r + 1] for r in range(8)],
                [[terms[c][r : r + 1] for r in range(8)] for c in range(3)],
            )
            return 0

        lax.fori_loop(0, ROWS // 8, body, 0)

    def elements(half):
        rows = slice(half * ROWS, (half + 1) * ROWS)
        columns = []
        for c in range(3):
            packed = nodal[c, rows, :]
            turned = pltpu.roll(packed, 64, 1)
            columns.append(jnp.concatenate([packed, turned], axis=0))
        top, rest = split(jnp.concatenate(columns, axis=1))
        gref = jnp.dot(
            fwd[...], jnp.concatenate([top, top, rest], axis=0), preferred_element_type=F32
        )
        jacobian = jac[...]
        lam = first[...]
        mu = shear[...]
        if half == 1:
            jacobian = pltpu.roll(jacobian, 64, 1)
            lam = pltpu.roll(lam, 64, 1)
            mu = pltpu.roll(mu, 64, 1)
        factor = [[jacobian[3 * r + i : 3 * r + i + 1] for i in range(3)] for r in range(3)]
        ref = [
            [
                gref[r * LANES : (r + 1) * LANES, c * LANES : (c + 1) * LANES]
                for r in range(3)
            ]
            for c in range(3)
        ]
        grad = [
            [
                factor[0][i] * ref[c][0] + factor[1][i] * ref[c][1] + factor[2][i] * ref[c][2]
                for i in range(3)
            ]
            for c in range(3)
        ]
        trace = lam * (grad[0][0] + grad[1][1] + grad[2][2])
        stress = [[None] * 3 for _ in range(3)]
        for c in range(3):
            stress[c][c] = 2.0 * mu * grad[c][c] + trace
            for i in range(c + 1, 3):
                stress[c][i] = stress[i][c] = mu * (grad[c][i] + grad[i][c])
        tref = jnp.concatenate(
            [
                jnp.concatenate(
                    [
                        factor[r][0] * stress[c][0]
                        + factor[r][1] * stress[c][1]
                        + factor[r][2] * stress[c][2]
                        for c in range(3)
                    ],
                    axis=1,
                )
                for r in range(3)
            ],
            axis=0,
        )
        top, rest = split(tref)
        result = jnp.dot(
            bwd[...], jnp.concatenate([top, top, rest], axis=0), preferred_element_type=F32
        )
        for c in range(3):
            part = result[:, c * LANES : (c + 1) * LANES]
            nodal[c, rows, :] = jnp.where(
                lane64 < 64, part[:ROWS], pltpu.roll(part[ROWS:], 64, 1)
            )

    gather(0)

    for copy in sends:
        copy.wait()
    for j in range(n_dom // 2):
        for c in range(3):
            tab[c, owned + j : owned + j + 1, :] = jnp.where(
                lane < 64, far_in[2 * j, c : c + 1, :], far_in[2 * j + 1, c : c + 1, :]
            )
    turn()
    found = pick(table[...], near_rows)
    for t in range(n_peers):
        for c in range(3):
            near_out[t, c : c + 1, :] = found[c][t]
    near_in[peer] = near_out[peer]
    sends = near_copies(near_out, near_in, send_near, recv_near)
    for copy in sends:
        copy.start()

    elements(0)

    for copy in sends:
        copy.wait()
    for c in range(3):
        tab[c, owned:, :] = jnp.zeros((LANES - owned, LANES), F32)
        for s in range(n_peers):
            tab[c, owned + s : owned + s + 1, :] = near_in[s, c : c + 1, :]
    turn()
    gather(1)
    elements(1)
    scatter(1, acc_out)
    outer = acc_out[...]
    kept = owned // 2
    for c in range(3):
        whole = joined(outer, c)
        for s in range(n_peers):
            half = (s % 2) * LANES
            ghost_out[s, c : c + 1, :] = whole[kept + s // 2 : kept + s // 2 + 1, half : half + LANES]
    ghost_in[peer] = ghost_out[peer]
    sends = near_copies(ghost_out, ghost_in, send_ghost, recv_ghost)
    for copy in sends:
        copy.start()

    scatter(0, acc_in)

    for copy in sends:
        copy.wait()
    ghost = spread(
        near_rows, [[ghost_in[t, c : c + 1, :] for t in range(n_peers)] for c in range(3)]
    )
    for c in range(3):
        whole = joined(ghost, c)
        for p in range(n_dom):
            half = ((p // 2) % 2) * LANES
            back_out[p, c : c + 1, :] = whole[kept + p // 4 : kept + p // 4 + 1, half : half + LANES]
    sends = far_copies(back_out, back_in, send_back, recv_back)
    for copy in sends:
        copy.start()
    total = acc_in[...] + acc_out[...] + ghost
    mine = (lane >> 6) == lax.rem(dom, 2)
    back_rows = [jnp.where(mine, far_rows[p], NOWHERE) for p in range(n_dom)]
    for copy in sends:
        copy.wait()
    total = total + spread(
        back_rows, [[back_in[p, c : c + 1, :] for p in range(n_dom)] for c in range(3)]
    )
    for c in range(3):
        whole = joined(total, c)
        for q in range(kept):
            out[c : c + 1, q * 2 * LANES : (q + 1) * 2 * LANES] = whole[q : q + 1]


def local(
    n_dom,
    n_sub,
    n_comp,
    displacement,
    far_lists,
    far_counts,
    near_lists,
    near_counts,
    connectivity,
    inverse_jacobian,
    lame_first,
    lame_shear,
):
    n_peers = n_sub * n_comp
    fwd, bwd = split_tables()
    smem = pl.BlockSpec(memory_space=pltpu.SMEM)
    vmem = pl.BlockSpec(memory_space=pltpu.VMEM)
    far_slots = pltpu.VMEM((n_dom, 8, LANES), F32)
    near_slots = pltpu.VMEM((n_peers, 8, LANES), F32)
    return pl.pallas_call(
        functools.partial(kernel, n_dom, n_sub, n_comp),
        out_shape=jax.ShapeDtypeStruct(displacement.shape, F32),
        in_specs=[smem] * 2 + [vmem] * 9,
        out_specs=vmem,
        scratch_shapes=[
            pltpu.VMEM((3, LANES, LANES), F32),
            pltpu.VMEM((3 * LANES, 2 * LANES), BF16),
            pltpu.VMEM((max(8, n_dom), LANES), jnp.int32),
            pltpu.VMEM((2, 2 * ROWS, LANES), jnp.int32),
            pltpu.VMEM((3, 2 * ROWS, LANES), F32),
            pltpu.VMEM((LANES, LANES), F32),
            pltpu.VMEM((LANES, LANES), F32),
            pltpu.VMEM((6 * HIGH, 2 * LANES), F32),
            pltpu.VMEM((6 * HIGH, 2 * LANES), F32),
            far_slots,
            far_slots,
            near_slots,
            near_slots,
            near_slots,
            near_slots,
            far_slots,
            far_slots,
        ]
        + [pltpu.SemaphoreType.DMA((n_dom,))] * 2
        + [pltpu.SemaphoreType.DMA((n_peers,))] * 4
        + [pltpu.SemaphoreType.DMA((n_dom,))] * 2,
        compiler_params=pltpu.CompilerParams(
            collective_id=0, has_side_effects=True, vmem_limit_bytes=32 * 1024 * 1024
        ),
    )(
        far_counts,
        near_counts,
        displacement,
        far_lists,
        near_lists,
        connectivity,
        inverse_jacobian,
        lame_first,
        lame_shear,
        jnp.asarray(fwd),
        jnp.asarray(bwd),
    )


def solution(mesh):
    spread_axes = ("groups", "dom", "sub", "comp")
    rows = P(spread_axes, None)
    columns = P(None, spread_axes)
    flat = P(spread_axes)
    in_specs = (columns, rows, flat, rows, flat, columns, columns, columns, columns)
    sizes = (mesh.shape["dom"], mesh.shape["sub"], mesh.shape["comp"])
    return jax.shard_map(
        functools.partial(local, *sizes),
        mesh=mesh,
        in_specs=in_specs,
        out_specs=columns,
        check_vma=False,
    )
```

```python
import functools
import math

import jax
import jax.numpy as jnp
import numpy as np
from jax import lax
from jax.experimental import pallas as pl
from jax.experimental.pallas import tpu as pltpu
from jax.sharding import PartitionSpec as P

F32 = jnp.float32
BF16 = jnp.bfloat16
LANES = 128
ROWS = 64
NOWHERE = 16383
HIGH = 48
MESH = pl.DeviceIdType.MESH


def basis_tables():
    gll_points = np.array([-1.0, -math.sqrt(3.0 / 7.0), 0.0, math.sqrt(3.0 / 7.0), 1.0])
    inner_root = math.sqrt(5.0 - 2.0 * math.sqrt(10.0 / 7.0)) / 3.0
    outer_root = math.sqrt(5.0 + 2.0 * math.sqrt(10.0 / 7.0)) / 3.0
    gauss_points = np.array([-outer_root, -inner_root, 0.0, inner_root, outer_root])
    values = np.zeros((5, 5))
    slopes = np.zeros((5, 5))
    for q in range(5):
        for n in range(5):
            product = 1.0
            for m in range(5):
                if m != n:
                    product = (
                        product
                        * (gauss_points[q] - gll_points[m])
                        / (gll_points[n] - gll_points[m])
                    )
            values[q, n] = product
            total = 0.0
            for l in range(5):
                if l != n:
                    term = 1.0 / (gll_points[n] - gll_points[l])
                    for m in range(5):
                        if m != n and m != l:
                            term = (
                                term
                                * (gauss_points[q] - gll_points[m])
                                / (gll_points[n] - gll_points[m])
                            )
                    total = total + term
            slopes[q, n] = total
    return (values, slopes)


def split_tables():
    values, slopes = basis_tables()
    forward = np.zeros((3, LANES, LANES), np.float32)
    for r in range(3):
        factors = [slopes if d == r else values for d in range(3)]
        forward[r, :125, :125] = np.kron(np.kron(factors[0], factors[1]), factors[2])
    stacked = forward.reshape(3 * LANES, LANES)
    top = stacked.astype(jnp.bfloat16)
    rest = (stacked - top.astype(np.float32)).astype(jnp.bfloat16)
    fwd = np.concatenate([top, rest, top], axis=1)
    bwd = np.concatenate([top.T, rest.T, top.T], axis=1)
    return np.ascontiguousarray(fwd), np.ascontiguousarray(bwd)


def split(x):
    top = x.astype(BF16)
    return top, (x - top.astype(F32)).astype(BF16)


def onehot(rows, key):
    grid = lax.broadcasted_iota(jnp.int32, (rows, key.shape[1]), 0)
    return jnp.where(grid == key, 1.0, 0.0).astype(BF16)


def pick(table, rows):
    found = [[], [], []]
    for at in range(0, len(rows), 2):
        pair = jnp.concatenate(rows[at : at + 2], axis=1)
        high = onehot(LANES, pair >> 7)
        dense = jnp.dot(
            table, jnp.concatenate([high, high], axis=0), preferred_element_type=F32
        )
        low = lax.broadcasted_iota(jnp.int32, (LANES, 2 * LANES), 0) == (pair & 127)
        for c in range(3):
            part = dense[c * LANES : (c + 1) * LANES]
            line = jnp.sum(jnp.where(low, part, 0.0), axis=0, keepdims=True)
            found[c] += [line[:, :LANES], line[:, LANES:]]
    return found


def spread(rows, values):
    key = jnp.concatenate(rows, axis=1)
    low = onehot(2 * LANES, key & 255)
    high = onehot(HIGH, key >> 8)
    parts = []
    for c in range(3):
        top, rest = split(jnp.concatenate(values[c], axis=1))
        parts += [high * top, high * rest]
    return lax.dot_general(
        jnp.concatenate(parts, axis=0),
        low,
        (((1,), (1,)), ((), ())),
        preferred_element_type=F32,
    )


def joined(acc, c):
    return acc[2 * HIGH * c : 2 * HIGH * c + HIGH] + acc[2 * HIGH * c + HIGH : 2 * HIGH * (c + 1)]


def kernel(
    n_dom,
    n_sub,
    n_comp,
    *refs,
):
    sources = refs[:11]
    loads = refs[-1]
    landed = refs[12:23]
    copies = [
        pltpu.make_async_copy(source, target, loads.at[at])
        for at, (source, target) in enumerate(zip(sources, landed))
    ]
    for copy in copies:
        copy.start()
    body(n_dom, n_sub, n_comp, copies, *landed, refs[11], *refs[23:-1])


def body(
    n_dom,
    n_sub,
    n_comp,
    copies,
    far_counts,
    near_counts,
    disp,
    far_lists,
    near_lists,
    conn,
    jac,
    lame_first,
    lame_shear,
    fwd,
    bwd,
    out,
    tab,
    table,
    far_index,
    index,
    nodal,
    first,
    shear,
    acc_in,
    acc_out,
    far_out,
    far_in,
    near_out,
    near_in,
    ghost_out,
    ghost_in,
    back_out,
    back_in,
    send_far,
    recv_far,
    send_near,
    recv_near,
    send_ghost,
    recv_ghost,
    send_back,
    recv_back,
):
    n_peers = n_sub * n_comp
    owned = disp.shape[1] // LANES
    dom = lax.axis_index("dom")
    peer = lax.axis_index("sub") * n_comp + lax.axis_index("comp")

    def dom_id(step):
        return {"dom": lax.rem(dom + step, n_dom)}

    def peer_id(step):
        other = lax.rem(peer + step, n_peers)
        return {"sub": other // n_comp, "comp": lax.rem(other, n_comp)}

    def far_copies(source, target, send, recv):
        return [
            pltpu.make_async_remote_copy(
                src_ref=source.at[lax.rem(dom + step, n_dom)],
                dst_ref=target.at[dom],
                send_sem=send.at[step],
                recv_sem=recv.at[step],
                device_id=dom_id(step),
                device_id_type=MESH,
            )
            for step in range(1, n_dom)
        ]

    def near_copies(source, target, send, recv):
        return [
            pltpu.make_async_remote_copy(
                src_ref=source.at[lax.rem(peer + step, n_peers)],
                dst_ref=target.at[peer],
                send_sem=send.at[step],
                recv_sem=recv.at[step],
                device_id=peer_id(step),
                device_id_type=MESH,
            )
            for step in range(1, n_peers)
        ]

    barrier = pltpu.get_barrier_semaphore()
    for step in range(1, n_dom):
        pl.semaphore_signal(barrier, inc=1, device_id=dom_id(step), device_id_type=MESH)
    for step in range(1, n_peers):
        pl.semaphore_signal(barrier, inc=1, device_id=peer_id(step), device_id_type=MESH)

    lane8 = lax.broadcasted_iota(jnp.int32, (8, LANES), 1)
    lane = lax.broadcasted_iota(jnp.int32, (1, LANES), 1)

    for copy in copies[:5]:
        copy.wait()

    for c in range(3):
        tab[c, owned:, :] = jnp.zeros((LANES - owned, LANES), F32)
        for h in range(owned):
            tab[c, h : h + 1, :] = disp[c : c + 1, h * LANES : (h + 1) * LANES]

    def turn():
        for c in range(3):
            top, rest = split(tab[c].T)
            table[c * LANES : (c + 1) * LANES, :LANES] = top
            table[c * LANES : (c + 1) * LANES, LANES:] = rest

    turn()

    far_index[...] = jnp.zeros_like(far_index)
    far_index[:n_dom, :64] = far_lists[...]
    listed = far_index[...]
    lane_f = lax.broadcasted_iota(jnp.int32, listed.shape, 1)
    listed = jnp.where(lane_f < 64, listed, pltpu.roll(listed, 64, 1))
    far_rows = [
        jnp.where((lane & 63) < far_counts[p], listed[p : p + 1], NOWHERE) for p in range(n_dom)
    ]
    near_rows = [
        jnp.where(lane < near_counts[t], near_lists[t : t + 1, :], NOWHERE)
        for t in range(n_peers)
    ]

    far_out[...] = jnp.zeros_like(far_out)
    near_out[...] = jnp.zeros_like(near_out)
    ghost_out[...] = jnp.zeros_like(ghost_out)
    back_out[...] = jnp.zeros_like(back_out)

    found = pick(table[...], far_rows)
    for p in range(n_dom):
        for c in range(3):
            far_out[p, c : c + 1, :] = found[c][p]
    far_in[dom] = jnp.zeros((8, LANES), F32)
    back_in[dom] = jnp.zeros((8, LANES), F32)

    pl.semaphore_wait(barrier, n_dom - 1 + n_peers - 1)
    sends = far_copies(far_out, far_in, send_far, recv_far)
    for copy in sends:
        copy.start()

    for copy in copies[5:]:
        copy.wait()

    tab_rows = jnp.full((8, LANES), NOWHERE, jnp.int32)
    index[0, 120:128, :] = tab_rows
    index[0, :125, :] = conn[...]
    low_half = index[0, :ROWS, :]
    high_half = index[0, ROWS:, :]
    lane64 = lax.broadcasted_iota(jnp.int32, (ROWS, LANES), 1)
    packed_in = jnp.where(lane64 < 64, low_half, pltpu.roll(high_half, 64, 1))
    packed_out = jnp.where(lane64 < 64, pltpu.roll(low_half, 64, 1), high_half)
    index[1, :ROWS, :] = packed_in
    index[1, ROWS:, :] = packed_out

    first[120:128, :] = jnp.zeros((8, LANES), F32)
    shear[120:128, :] = jnp.zeros((8, LANES), F32)
    first[:125, :] = lame_first[...].astype(F32)
    shear[:125, :] = lame_shear[...].astype(F32)

    def gather(half):
        def body(step, _):
            at = pl.multiple_of(half * ROWS + step * 8, 8)
            block = index[1, pl.ds(at, 8), :]
            got = pick(table[...], [block[r : r + 1] for r in range(8)])
            for c in range(3):
                nodal[c, pl.ds(at, 8), :] = jnp.concatenate(got[c], axis=0)
            return 0

        lax.fori_loop(0, ROWS // 8, body, 0)

    def scatter(half, acc):
        acc[...] = jnp.zeros_like(acc)

        def body(step, _):
            at = pl.multiple_of(half * ROWS + step * 8, 8)
            block = index[1, pl.ds(at, 8), :]
            terms = [nodal[c, pl.ds(at, 8), :] for c in range(3)]
            acc[...] += spread(
                [block[r : r + 1] for r in range(8)],
                [[terms[c][r : r + 1] for r in range(8)] for c in range(3)],
            )
            return 0

        lax.fori_loop(0, ROWS // 8, body, 0)

    def elements(half):
        rows = slice(half * ROWS, (half + 1) * ROWS)
        columns = []
        for c in range(3):
            packed = nodal[c, rows, :]
            turned = pltpu.roll(packed, 64, 1)
            columns.append(jnp.concatenate([packed, turned], axis=0))
        top, rest = split(jnp.concatenate(columns, axis=1))
        gref = jnp.dot(
            fwd[...], jnp.concatenate([top, top, rest], axis=0), preferred_element_type=F32
        )
        jacobian = jac[...]
        lam = first[...]
        mu = shear[...]
        if half == 1:
            jacobian = pltpu.roll(jacobian, 64, 1)
            lam = pltpu.roll(lam, 64, 1)
            mu = pltpu.roll(mu, 64, 1)
        factor = [[jacobian[3 * r + i : 3 * r + i + 1] for i in range(3)] for r in range(3)]
        ref = [
            [
                gref[r * LANES : (r + 1) * LANES, c * LANES : (c + 1) * LANES]
                for r in range(3)
            ]
            for c in range(3)
        ]
        grad = [
            [
                factor[0][i] * ref[c][0] + factor[1][i] * ref[c][1] + factor[2][i] * ref[c][2]
                for i in range(3)
            ]
            for c in range(3)
        ]
        trace = lam * (grad[0][0] + grad[1][1] + grad[2][2])
        stress = [[None] * 3 for _ in range(3)]
        for c in range(3):
            stress[c][c] = 2.0 * mu * grad[c][c] + trace
            for i in range(c + 1, 3):
                stress[c][i] = stress[i][c] = mu * (grad[c][i] + grad[i][c])
        tref = jnp.concatenate(
            [
                jnp.concatenate(
                    [
                        factor[r][0] * stress[c][0]
                        + factor[r][1] * stress[c][1]
                        + factor[r][2] * stress[c][2]
                        for c in range(3)
                    ],
                    axis=1,
                )
                for r in range(3)
            ],
            axis=0,
        )
        top, rest = split(tref)
        result = jnp.dot(
            bwd[...], jnp.concatenate([top, top, rest], axis=0), preferred_element_type=F32
        )
        for c in range(3):
            part = result[:, c * LANES : (c + 1) * LANES]
            nodal[c, rows, :] = jnp.where(
                lane64 < 64, part[:ROWS], pltpu.roll(part[ROWS:], 64, 1)
            )

    gather(0)

    for copy in sends:
        copy.wait()
    for j in range(n_dom // 2):
        for c in range(3):
            tab[c, owned + j : owned + j + 1, :] = jnp.where(
                lane < 64, far_in[2 * j, c : c + 1, :], far_in[2 * j + 1, c : c + 1, :]
            )
    turn()
    found = pick(table[...], near_rows)
    for t in range(n_peers):
        for c in range(3):
            near_out[t, c : c + 1, :] = found[c][t]
    near_in[peer] = near_out[peer]
    sends = near_copies(near_out, near_in, send_near, recv_near)
    for copy in sends:
        copy.start()

    elements(0)

    for copy in sends:
        copy.wait()
    for c in range(3):
        tab[c, owned:, :] = jnp.zeros((LANES - owned, LANES), F32)
        for s in range(n_peers):
            tab[c, owned + s : owned + s + 1, :] = near_in[s, c : c + 1, :]
    turn()
    gather(1)
    elements(1)
    scatter(1, acc_out)
    outer = acc_out[...]
    kept = owned // 2
    for c in range(3):
        whole = joined(outer, c)
        for s in range(n_peers):
            half = (s % 2) * LANES
            ghost_out[s, c : c + 1, :] = whole[kept + s // 2 : kept + s // 2 + 1, half : half + LANES]
    ghost_in[peer] = ghost_out[peer]
    sends = near_copies(ghost_out, ghost_in, send_ghost, recv_ghost)
    for copy in sends:
        copy.start()

    scatter(0, acc_in)

    for copy in sends:
        copy.wait()
    ghost = spread(
        near_rows, [[ghost_in[t, c : c + 1, :] for t in range(n_peers)] for c in range(3)]
    )
    for c in range(3):
        whole = joined(ghost, c)
        for p in range(n_dom):
            half = ((p // 2) % 2) * LANES
            back_out[p, c : c + 1, :] = whole[kept + p // 4 : kept + p // 4 + 1, half : half + LANES]
    sends = far_copies(back_out, back_in, send_back, recv_back)
    for copy in sends:
        copy.start()
    total = acc_in[...] + acc_out[...] + ghost
    mine = (lane >> 6) == lax.rem(dom, 2)
    back_rows = [jnp.where(mine, far_rows[p], NOWHERE) for p in range(n_dom)]
    for copy in sends:
        copy.wait()
    total = total + spread(
        back_rows, [[back_in[p, c : c + 1, :] for p in range(n_dom)] for c in range(3)]
    )
    for c in range(3):
        whole = joined(total, c)
        for q in range(kept):
            out[c : c + 1, q * 2 * LANES : (q + 1) * 2 * LANES] = whole[q : q + 1]


def local(
    n_dom,
    n_sub,
    n_comp,
    displacement,
    far_lists,
    far_counts,
    near_lists,
    near_counts,
    connectivity,
    inverse_jacobian,
    lame_first,
    lame_shear,
):
    n_peers = n_sub * n_comp
    fwd, bwd = split_tables()
    operands = (
        far_counts,
        near_counts,
        displacement,
        far_lists,
        near_lists,
        connectivity,
        inverse_jacobian,
        lame_first,
        lame_shear,
        jnp.asarray(fwd),
        jnp.asarray(bwd),
    )
    far_slots = pltpu.VMEM((n_dom, 8, LANES), F32)
    near_slots = pltpu.VMEM((n_peers, 8, LANES), F32)
    return pl.pallas_call(
        functools.partial(kernel, n_dom, n_sub, n_comp),
        out_shape=jax.ShapeDtypeStruct(displacement.shape, F32),
        in_specs=[pl.BlockSpec(memory_space=pltpu.HBM)] * 11,
        out_specs=pl.BlockSpec(memory_space=pltpu.VMEM),
        scratch_shapes=[
            pltpu.SMEM(operands[0].shape, jnp.int32),
            pltpu.SMEM(operands[1].shape, jnp.int32),
        ]
        + [pltpu.VMEM(x.shape, x.dtype) for x in operands[2:]]
        + [
            pltpu.VMEM((3, LANES, LANES), F32),
            pltpu.VMEM((3 * LANES, 2 * LANES), BF16),
            pltpu.VMEM((max(8, n_dom), LANES), jnp.int32),
            pltpu.VMEM((2, 2 * ROWS, LANES), jnp.int32),
            pltpu.VMEM((3, 2 * ROWS, LANES), F32),
            pltpu.VMEM((LANES, LANES), F32),
            pltpu.VMEM((LANES, LANES), F32),
            pltpu.VMEM((6 * HIGH, 2 * LANES), F32),
            pltpu.VMEM((6 * HIGH, 2 * LANES), F32),
            far_slots,
            far_slots,
            near_slots,
            near_slots,
            near_slots,
            near_slots,
            far_slots,
            far_slots,
        ]
        + [pltpu.SemaphoreType.DMA((n_dom,))] * 2
        + [pltpu.SemaphoreType.DMA((n_peers,))] * 4
        + [pltpu.SemaphoreType.DMA((n_dom,))] * 2
        + [pltpu.SemaphoreType.DMA((11,))],
        compiler_params=pltpu.CompilerParams(
            collective_id=0, has_side_effects=True, vmem_limit_bytes=32 * 1024 * 1024
        ),
    )(*operands)


def solution(mesh):
    spread_axes = ("groups", "dom", "sub", "comp")
    rows = P(spread_axes, None)
    columns = P(None, spread_axes)
    flat = P(spread_axes)
    in_specs = (columns, rows, flat, rows, flat, columns, columns, columns, columns)
    sizes = (mesh.shape["dom"], mesh.shape["sub"], mesh.shape["comp"])
    return jax.shard_map(
        functools.partial(local, *sizes),
        mesh=mesh,
        in_specs=in_specs,
        out_specs=columns,
        check_vma=False,
    )
```

```python
import functools
import math

import jax
import jax.numpy as jnp
import numpy as np
from jax import lax
from jax.experimental import pallas as pl
from jax.experimental.pallas import tpu as pltpu
from jax.sharding import PartitionSpec as P

F32 = jnp.float32
BF16 = jnp.bfloat16
LANES = 128
CAP_FAR = 64
ROWS = 64
NOWHERE = 1 << 20
HIGH = 48
MESH = pl.DeviceIdType.MESH


def basis_tables():
    gll_points = np.array([-1.0, -math.sqrt(3.0 / 7.0), 0.0, math.sqrt(3.0 / 7.0), 1.0])
    inner_root = math.sqrt(5.0 - 2.0 * math.sqrt(10.0 / 7.0)) / 3.0
    outer_root = math.sqrt(5.0 + 2.0 * math.sqrt(10.0 / 7.0)) / 3.0
    gauss_points = np.array([-outer_root, -inner_root, 0.0, inner_root, outer_root])
    values = np.zeros((5, 5))
    slopes = np.zeros((5, 5))
    for q in range(5):
        for n in range(5):
            product = 1.0
            for m in range(5):
                if m != n:
                    product = (
                        product
                        * (gauss_points[q] - gll_points[m])
                        / (gll_points[n] - gll_points[m])
                    )
            values[q, n] = product
            total = 0.0
            for l in range(5):
                if l != n:
                    term = 1.0 / (gll_points[n] - gll_points[l])
                    for m in range(5):
                        if m != n and m != l:
                            term = (
                                term
                                * (gauss_points[q] - gll_points[m])
                                / (gll_points[n] - gll_points[m])
                            )
                    total = total + term
            slopes[q, n] = total
    return (values, slopes)


def split_tables():
    values, slopes = basis_tables()
    forward = np.zeros((3, LANES, LANES), np.float32)
    for r in range(3):
        factors = [slopes if d == r else values for d in range(3)]
        forward[r, :125, :125] = np.kron(np.kron(factors[0], factors[1]), factors[2])
    stacked = forward.reshape(3 * LANES, LANES)
    top = stacked.astype(jnp.bfloat16)
    rest = (stacked - top.astype(np.float32)).astype(jnp.bfloat16)
    fwd = np.concatenate([top, rest, top], axis=1)
    bwd = np.concatenate([top.T, rest.T, top.T], axis=1)
    return np.ascontiguousarray(fwd), np.ascontiguousarray(bwd)


def split(x):
    top = x.astype(BF16)
    return top, (x - top.astype(F32)).astype(BF16)


def onehot(rows, key):
    grid = lax.broadcasted_iota(jnp.int32, (rows, key.shape[1]), 0)
    return jnp.where(grid == key, 1.0, 0.0).astype(BF16)


def pick(table, rows):
    found = [[], [], []]
    for at in range(0, len(rows), 2):
        pair = jnp.concatenate(rows[at : at + 2], axis=1)
        high = onehot(LANES, pair >> 7)
        dense = jnp.dot(
            table, jnp.concatenate([high, high], axis=0), preferred_element_type=F32
        )
        low = lax.broadcasted_iota(jnp.int32, (LANES, 2 * LANES), 0) == (pair & 127)
        for c in range(3):
            part = dense[c * LANES : (c + 1) * LANES]
            line = jnp.sum(jnp.where(low, part, 0.0), axis=0, keepdims=True)
            found[c] += [line[:, :LANES], line[:, LANES:]]
    return found


def spread(rows, values, height=HIGH):
    key = jnp.concatenate(rows, axis=1)
    low = onehot(2 * LANES, key & 255)
    high = onehot(height, key >> 8)
    parts = []
    for c in range(3):
        top, rest = split(jnp.concatenate(values[c], axis=1))
        parts += [high * top, high * rest]
    return lax.dot_general(
        jnp.concatenate(parts, axis=0),
        low,
        (((1,), (1,)), ((), ())),
        preferred_element_type=F32,
    )


def joined(acc, c, height=HIGH):
    start = 2 * height * c
    return acc[start : start + height] + acc[start + height : start + 2 * height]


def kernel(
    n_dom,
    n_sub,
    n_comp,
    *refs,
):
    sources = refs[:11]
    loads = refs[-1]
    landed = refs[12:23]
    copies = [
        pltpu.make_async_copy(source, target, loads.at[at])
        for at, (source, target) in enumerate(zip(sources, landed))
    ]
    for copy in copies:
        copy.start()
    body(n_dom, n_sub, n_comp, copies, *landed, refs[11], *refs[23:-1])


def body(
    n_dom,
    n_sub,
    n_comp,
    copies,
    far_counts,
    near_counts,
    disp,
    far_lists,
    near_lists,
    conn,
    jac,
    lame_first,
    lame_shear,
    fwd,
    bwd,
    out,
    tab,
    table,
    far_tab,
    far_table,
    far_index,
    index,
    nodal,
    first,
    shear,
    acc_in,
    acc_out,
    far_out,
    far_in,
    near_out,
    near_in,
    ghost_out,
    ghost_in,
    back_out,
    back_in,
    send_far,
    recv_far,
    send_near,
    recv_near,
    send_ghost,
    recv_ghost,
    send_back,
    recv_back,
):
    n_peers = n_sub * n_comp
    node_count = disp.shape[1]
    owned = node_count // LANES
    dom = lax.axis_index("dom")
    peer = lax.axis_index("sub") * n_comp + lax.axis_index("comp")

    far_rows_each = n_dom * CAP_FAR // LANES
    others = [(d, t) for d in range(1, n_dom) for t in range(n_peers)]

    def near_id(step):
        other = lax.rem(peer + step, n_peers)
        return {"sub": other // n_comp, "comp": lax.rem(other, n_comp)}

    def near_copies(source, target, send, recv):
        return [
            pltpu.make_async_remote_copy(
                src_ref=source.at[lax.rem(peer + step, n_peers)],
                dst_ref=target.at[peer],
                send_sem=send.at[step],
                recv_sem=recv.at[step],
                device_id=near_id(step),
                device_id_type=MESH,
            )
            for step in range(1, n_peers)
        ]

    def far_copies(source_at, target_at, send, recv):
        return [
            pltpu.make_async_remote_copy(
                src_ref=source_at(d, lax.rem(peer + t, n_peers)),
                dst_ref=target_at,
                send_sem=send.at[d * n_peers + t],
                recv_sem=recv.at[d * n_peers + t],
                device_id=dict(near_id(t), dom=lax.rem(dom + d, n_dom)),
                device_id_type=MESH,
            )
            for d, t in others
        ]

    barrier = pltpu.get_barrier_semaphore()
    for d in range(n_dom):
        for t in range(n_peers):
            if d or t:
                pl.semaphore_signal(
                    barrier,
                    inc=1,
                    device_id=dict(near_id(t), dom=lax.rem(dom + d, n_dom)),
                    device_id_type=MESH,
                )

    lane = lax.broadcasted_iota(jnp.int32, (1, LANES), 1)

    for copy in copies[:5]:
        copy.wait()

    for c in range(3):
        tab[c, owned:, :] = jnp.zeros((LANES - owned, LANES), F32)
        for h in range(owned):
            tab[c, h : h + 1, :] = disp[c : c + 1, h * LANES : (h + 1) * LANES]

    def turn(source, table):
        for c in range(3):
            top, rest = split(source[c].T)
            table[c * LANES : (c + 1) * LANES, :LANES] = top
            table[c * LANES : (c + 1) * LANES, LANES:] = rest

    turn(tab, table)

    far_index[...] = jnp.zeros_like(far_index)
    far_index[:n_dom, :64] = far_lists[...]
    listed = far_index[...]
    lane_f = lax.broadcasted_iota(jnp.int32, listed.shape, 1)
    listed = jnp.where(lane_f < 64, listed, pltpu.roll(listed, 64, 1))
    far_rows = [
        jnp.where((lane & 63) < far_counts[p], listed[p : p + 1], NOWHERE) for p in range(n_dom)
    ]
    near_rows = [
        jnp.where(lane < near_counts[t], near_lists[t : t + 1, :], NOWHERE)
        for t in range(n_peers)
    ]

    own_rows = [jnp.where(row < node_count, row, NOWHERE) for row in near_rows]
    far_keys = [
        jnp.where(
            (row >= node_count) & (row < NOWHERE),
            row + (peer * (n_dom * CAP_FAR) - node_count),
            NOWHERE,
        )
        for row in near_rows
    ]

    far_out[...] = jnp.zeros_like(far_out)
    near_out[...] = jnp.zeros_like(near_out)
    ghost_out[...] = jnp.zeros_like(ghost_out)
    back_out[...] = jnp.zeros_like(back_out)

    found = pick(table[...], far_rows + own_rows)
    for p in range(n_dom):
        for c in range(3):
            far_out[p, c : c + 1, :] = found[c][p]
    for t in range(n_peers):
        for c in range(3):
            near_out[t, c : c + 1, :] = found[c][n_dom + t]
        near_out[t, 3:4, :] = far_keys[t].astype(F32)
    for s in range(n_peers):
        far_in[s, dom] = jnp.zeros((8, LANES), F32)
        back_in[dom, s] = jnp.zeros((8, LANES), F32)

    pl.semaphore_wait(barrier, n_dom * n_peers - 1)
    far_sends = far_copies(
        lambda d, t: far_out.at[lax.rem(dom + d, n_dom)],
        far_in.at[peer, dom],
        send_far,
        recv_far,
    )
    near_sends = near_copies(near_out, near_in, send_near, recv_near)
    for copy in far_sends + near_sends:
        copy.start()
    near_in[peer] = near_out[peer]

    for copy in copies[5:]:
        copy.wait()

    tab_rows = jnp.full((8, LANES), NOWHERE, jnp.int32)
    index[0, 120:128, :] = tab_rows
    index[0, :125, :] = conn[...]
    low_half = index[0, :ROWS, :]
    high_half = index[0, ROWS:, :]
    lane64 = lax.broadcasted_iota(jnp.int32, (ROWS, LANES), 1)
    packed_in = jnp.where(lane64 < 64, low_half, pltpu.roll(high_half, 64, 1))
    packed_out = jnp.where(lane64 < 64, pltpu.roll(low_half, 64, 1), high_half)
    index[1, :ROWS, :] = packed_in
    index[1, ROWS:, :] = packed_out

    first[120:128, :] = jnp.zeros((8, LANES), F32)
    shear[120:128, :] = jnp.zeros((8, LANES), F32)
    first[:125, :] = lame_first[...].astype(F32)
    shear[:125, :] = lame_shear[...].astype(F32)

    def gather(half):
        def body(step, _):
            at = pl.multiple_of(half * ROWS + step * 8, 8)
            block = index[1, pl.ds(at, 8), :]
            got = pick(table[...], [block[r : r + 1] for r in range(8)])
            for c in range(3):
                nodal[c, pl.ds(at, 8), :] = jnp.concatenate(got[c], axis=0)
            return 0

        lax.fori_loop(0, ROWS // 8, body, 0)

    def scatter(half, acc):
        acc[...] = jnp.zeros_like(acc)

        def body(step, _):
            at = pl.multiple_of(half * ROWS + step * 8, 8)
            block = index[1, pl.ds(at, 8), :]
            terms = [nodal[c, pl.ds(at, 8), :] for c in range(3)]
            acc[...] += spread(
                [block[r : r + 1] for r in range(8)],
                [[terms[c][r : r + 1] for r in range(8)] for c in range(3)],
            )
            return 0

        lax.fori_loop(0, ROWS // 8, body, 0)

    def elements(half):
        rows = slice(half * ROWS, (half + 1) * ROWS)
        columns = []
        for c in range(3):
            packed = nodal[c, rows, :]
            turned = pltpu.roll(packed, 64, 1)
            columns.append(jnp.concatenate([packed, turned], axis=0))
        top, rest = split(jnp.concatenate(columns, axis=1))
        gref = jnp.dot(
            fwd[...], jnp.concatenate([top, top, rest], axis=0), preferred_element_type=F32
        )
        jacobian = jac[...]
        lam = first[...]
        mu = shear[...]
        if half == 1:
            jacobian = pltpu.roll(jacobian, 64, 1)
            lam = pltpu.roll(lam, 64, 1)
            mu = pltpu.roll(mu, 64, 1)
        factor = [[jacobian[3 * r + i : 3 * r + i + 1] for i in range(3)] for r in range(3)]
        ref = [
            [
                gref[r * LANES : (r + 1) * LANES, c * LANES : (c + 1) * LANES]
                for r in range(3)
            ]
            for c in range(3)
        ]
        grad = [
            [
                factor[0][i] * ref[c][0] + factor[1][i] * ref[c][1] + factor[2][i] * ref[c][2]
                for i in range(3)
            ]
            for c in range(3)
        ]
        trace = lam * (grad[0][0] + grad[1][1] + grad[2][2])
        stress = [[None] * 3 for _ in range(3)]
        for c in range(3):
            stress[c][c] = 2.0 * mu * grad[c][c] + trace
            for i in range(c + 1, 3):
                stress[c][i] = stress[i][c] = mu * (grad[c][i] + grad[i][c])
        tref = jnp.concatenate(
            [
                jnp.concatenate(
                    [
                        factor[r][0] * stress[c][0]
                        + factor[r][1] * stress[c][1]
                        + factor[r][2] * stress[c][2]
                        for c in range(3)
                    ],
                    axis=1,
                )
                for r in range(3)
            ],
            axis=0,
        )
        top, rest = split(tref)
        result = jnp.dot(
            bwd[...], jnp.concatenate([top, top, rest], axis=0), preferred_element_type=F32
        )
        for c in range(3):
            part = result[:, c * LANES : (c + 1) * LANES]
            nodal[c, rows, :] = jnp.where(
                lane64 < 64, part[:ROWS], pltpu.roll(part[ROWS:], 64, 1)
            )

    gather(0)

    elements(0)

    far_tab[...] = jnp.zeros_like(far_tab)
    for copy in far_sends + near_sends:
        copy.wait()
    for s in range(n_peers):
        for j in range(far_rows_each):
            at = s * far_rows_each + j
            for c in range(3):
                far_tab[c, at : at + 1, :] = jnp.where(
                    lane < 64, far_in[s, 2 * j, c : c + 1, :], far_in[s, 2 * j + 1, c : c + 1, :]
                )
    turn(far_tab, far_table)
    ghost_keys = [near_in[s, 3:4, :].astype(jnp.int32) for s in range(n_peers)]
    found = pick(far_table[...], ghost_keys)
    for c in range(3):
        for s in range(n_peers):
            tab[c, owned + s : owned + s + 1, :] = near_in[s, c : c + 1, :] + found[c][s]
    turn(tab, table)
    gather(1)
    elements(1)
    scatter(1, acc_out)
    outer = acc_out[...]
    kept = owned // 2
    for c in range(3):
        whole = joined(outer, c)
        for s in range(n_peers):
            half = (s % 2) * LANES
            ghost_out[s, c : c + 1, :] = whole[kept + s // 2 : kept + s // 2 + 1, half : half + LANES]
    far_height = -(-n_peers * n_dom * CAP_FAR // (2 * LANES) // 16) * 16
    beyond = spread(
        ghost_keys,
        [[ghost_out[s, c : c + 1, :] for s in range(n_peers)] for c in range(3)],
        far_height,
    )
    for c in range(3):
        whole = joined(beyond, c, far_height)
        for s in range(n_peers):
            for p in range(n_dom):
                row = s * (far_rows_each // 2) + p // 4
                half = ((p // 2) % 2) * LANES
                back_out[p, s, c : c + 1, :] = whole[row : row + 1, half : half + LANES]
    sends = near_copies(ghost_out, ghost_in, send_ghost, recv_ghost) + far_copies(
        lambda d, t: back_out.at[lax.rem(dom + d, n_dom), t],
        back_in.at[dom, peer],
        send_back,
        recv_back,
    )
    for copy in sends:
        copy.start()
    ghost_in[peer] = ghost_out[peer]

    scatter(0, acc_in)
    mine = (lane >> 6) == lax.rem(dom, 2)
    back_rows = [jnp.where(mine, far_rows[p], NOWHERE) for p in range(n_dom)]

    for copy in sends:
        copy.wait()
    arrived = [back_in[p, 0] for p in range(n_dom)]
    for t in range(1, n_peers):
        arrived = [arrived[p] + back_in[p, t] for p in range(n_dom)]
    total = acc_in[...] + acc_out[...]
    total = total + spread(
        own_rows + back_rows,
        [
            [ghost_in[t, c : c + 1, :] for t in range(n_peers)]
            + [arrived[p][c : c + 1, :] for p in range(n_dom)]
            for c in range(3)
        ],
    )
    for c in range(3):
        whole = joined(total, c)
        for q in range(kept):
            out[c : c + 1, q * 2 * LANES : (q + 1) * 2 * LANES] = whole[q : q + 1]


def local(
    n_dom,
    n_sub,
    n_comp,
    displacement,
    far_lists,
    far_counts,
    near_lists,
    near_counts,
    connectivity,
    inverse_jacobian,
    lame_first,
    lame_shear,
):
    n_peers = n_sub * n_comp
    fwd, bwd = split_tables()
    operands = (
        far_counts,
        near_counts,
        displacement,
        far_lists,
        near_lists,
        connectivity,
        inverse_jacobian,
        lame_first,
        lame_shear,
        jnp.asarray(fwd),
        jnp.asarray(bwd),
    )
    near_slots = pltpu.VMEM((n_peers, 8, LANES), F32)
    return pl.pallas_call(
        functools.partial(kernel, n_dom, n_sub, n_comp),
        out_shape=jax.ShapeDtypeStruct(displacement.shape, F32),
        in_specs=[pl.BlockSpec(memory_space=pltpu.HBM)] * 11,
        out_specs=pl.BlockSpec(memory_space=pltpu.VMEM),
        scratch_shapes=[
            pltpu.SMEM(operands[0].shape, jnp.int32),
            pltpu.SMEM(operands[1].shape, jnp.int32),
        ]
        + [pltpu.VMEM(x.shape, x.dtype) for x in operands[2:]]
        + [
            pltpu.VMEM((3, LANES, LANES), F32),
            pltpu.VMEM((3 * LANES, 2 * LANES), BF16),
            pltpu.VMEM((3, LANES, LANES), F32),
            pltpu.VMEM((3 * LANES, 2 * LANES), BF16),
            pltpu.VMEM((max(8, n_dom), LANES), jnp.int32),
            pltpu.VMEM((2, 2 * ROWS, LANES), jnp.int32),
            pltpu.VMEM((3, 2 * ROWS, LANES), F32),
            pltpu.VMEM((LANES, LANES), F32),
            pltpu.VMEM((LANES, LANES), F32),
            pltpu.VMEM((6 * HIGH, 2 * LANES), F32),
            pltpu.VMEM((6 * HIGH, 2 * LANES), F32),
            pltpu.VMEM((n_dom, 8, LANES), F32),
            pltpu.VMEM((n_peers, n_dom, 8, LANES), F32),
            near_slots,
            near_slots,
            near_slots,
            near_slots,
            pltpu.VMEM((n_dom, n_peers, 8, LANES), F32),
            pltpu.VMEM((n_dom, n_peers, 8, LANES), F32),
        ]
        + [pltpu.SemaphoreType.DMA((n_dom * n_peers,))] * 2
        + [pltpu.SemaphoreType.DMA((n_peers,))] * 4
        + [pltpu.SemaphoreType.DMA((n_dom * n_peers,))] * 2
        + [pltpu.SemaphoreType.DMA((11,))],
        compiler_params=pltpu.CompilerParams(
            collective_id=0, has_side_effects=True
        ),
    )(*operands)


def solution(mesh):
    spread_axes = ("groups", "dom", "sub", "comp")
    rows = P(spread_axes, None)
    columns = P(None, spread_axes)
    flat = P(spread_axes)
    in_specs = (columns, rows, flat, rows, flat, columns, columns, columns, columns)
    sizes = (mesh.shape["dom"], mesh.shape["sub"], mesh.shape["comp"])
    return jax.shard_map(
        functools.partial(local, *sizes),
        mesh=mesh,
        in_specs=in_specs,
        out_specs=columns,
        check_vma=False,
    )
```

```python
import functools
import math

import jax
import jax.numpy as jnp
import numpy as np
from jax import lax
from jax.experimental import pallas as pl
from jax.experimental.pallas import tpu as pltpu
from jax.sharding import PartitionSpec as P

F32 = jnp.float32
BF16 = jnp.bfloat16
LANES = 128
CAP_FAR = 64
ROWS = 64
NOWHERE = 1 << 20
HIGH = 48
MESH = pl.DeviceIdType.MESH


def basis_tables():
    gll_points = np.array([-1.0, -math.sqrt(3.0 / 7.0), 0.0, math.sqrt(3.0 / 7.0), 1.0])
    inner_root = math.sqrt(5.0 - 2.0 * math.sqrt(10.0 / 7.0)) / 3.0
    outer_root = math.sqrt(5.0 + 2.0 * math.sqrt(10.0 / 7.0)) / 3.0
    gauss_points = np.array([-outer_root, -inner_root, 0.0, inner_root, outer_root])
    values = np.zeros((5, 5))
    slopes = np.zeros((5, 5))
    for q in range(5):
        for n in range(5):
            product = 1.0
            for m in range(5):
                if m != n:
                    product = (
                        product
                        * (gauss_points[q] - gll_points[m])
                        / (gll_points[n] - gll_points[m])
                    )
            values[q, n] = product
            total = 0.0
            for l in range(5):
                if l != n:
                    term = 1.0 / (gll_points[n] - gll_points[l])
                    for m in range(5):
                        if m != n and m != l:
                            term = (
                                term
                                * (gauss_points[q] - gll_points[m])
                                / (gll_points[n] - gll_points[m])
                            )
                    total = total + term
            slopes[q, n] = total
    return (values, slopes)


def split_tables():
    values, slopes = basis_tables()
    forward = np.zeros((3, LANES, LANES), np.float32)
    for r in range(3):
        factors = [slopes if d == r else values for d in range(3)]
        forward[r, :125, :125] = np.kron(np.kron(factors[0], factors[1]), factors[2])
    stacked = forward.reshape(3 * LANES, LANES)
    top = stacked.astype(jnp.bfloat16)
    rest = (stacked - top.astype(np.float32)).astype(jnp.bfloat16)
    fwd = np.concatenate([top, rest, top], axis=1)
    bwd = np.concatenate([top.T, rest.T, top.T], axis=1)
    return np.ascontiguousarray(fwd), np.ascontiguousarray(bwd)


def split(x):
    top = x.astype(BF16)
    return top, (x - top.astype(F32)).astype(BF16)


def onehot(rows, key):
    grid = lax.broadcasted_iota(jnp.int32, (rows, key.shape[1]), 0).astype(F32).astype(BF16)
    name = key.astype(F32).astype(BF16)
    return jnp.where(grid == name, jnp.ones((), BF16), jnp.zeros((), BF16))


def pick(table, rows):
    found = [[], [], []]
    for at in range(0, len(rows), 2):
        pair = jnp.concatenate(rows[at : at + 2], axis=1)
        high = onehot(LANES, pair >> 7)
        dense = jnp.dot(
            table, jnp.concatenate([high, high], axis=0), preferred_element_type=F32
        )
        low = lax.broadcasted_iota(jnp.int32, (LANES, 2 * LANES), 0) == (pair & 127)
        for c in range(3):
            part = dense[c * LANES : (c + 1) * LANES]
            line = jnp.sum(jnp.where(low, part, 0.0), axis=0, keepdims=True)
            found[c] += [line[:, :LANES], line[:, LANES:]]
    return found


def spread(rows, values, height=HIGH):
    key = jnp.concatenate(rows, axis=1)
    low = onehot(2 * LANES, key & 255)
    high = onehot(height, key >> 8)
    parts = []
    for c in range(3):
        top, rest = split(jnp.concatenate(values[c], axis=1))
        parts += [high * top, high * rest]
    return lax.dot_general(
        jnp.concatenate(parts, axis=0),
        low,
        (((1,), (1,)), ((), ())),
        preferred_element_type=F32,
    )


def joined(acc, c, height=HIGH):
    start = 2 * height * c
    return acc[start : start + height] + acc[start + height : start + 2 * height]


def kernel(
    n_dom,
    n_sub,
    n_comp,
    *refs,
):
    sources = refs[:11]
    loads = refs[-1]
    landed = refs[12:23]
    copies = [
        pltpu.make_async_copy(source, target, loads.at[at])
        for at, (source, target) in enumerate(zip(sources, landed))
    ]
    for copy in copies:
        copy.start()
    body(n_dom, n_sub, n_comp, copies, *landed, refs[11], *refs[23:-1])


def body(
    n_dom,
    n_sub,
    n_comp,
    copies,
    far_counts,
    near_counts,
    disp,
    far_lists,
    near_lists,
    conn,
    jac,
    lame_first,
    lame_shear,
    fwd,
    bwd,
    out,
    tab,
    table,
    far_tab,
    far_table,
    far_index,
    index,
    nodal,
    first,
    shear,
    acc_in,
    acc_out,
    far_out,
    far_in,
    near_out,
    near_in,
    ghost_out,
    ghost_in,
    back_out,
    back_in,
    send_far,
    recv_far,
    send_near,
    recv_near,
    send_ghost,
    recv_ghost,
    send_back,
    recv_back,
):
    n_peers = n_sub * n_comp
    node_count = disp.shape[1]
    owned = node_count // LANES
    dom = lax.axis_index("dom")
    peer = lax.axis_index("sub") * n_comp + lax.axis_index("comp")

    far_rows_each = n_dom * CAP_FAR // LANES
    others = [(d, t) for d in range(1, n_dom) for t in range(n_peers)]

    def near_id(step):
        other = lax.rem(peer + step, n_peers)
        return {"sub": other // n_comp, "comp": lax.rem(other, n_comp)}

    def near_copies(source, target, send, recv):
        return [
            pltpu.make_async_remote_copy(
                src_ref=source.at[lax.rem(peer + step, n_peers)],
                dst_ref=target.at[peer],
                send_sem=send.at[step],
                recv_sem=recv.at[step],
                device_id=near_id(step),
                device_id_type=MESH,
            )
            for step in range(1, n_peers)
        ]

    def far_copies(source_at, target_at, send, recv):
        return [
            pltpu.make_async_remote_copy(
                src_ref=source_at(d, lax.rem(peer + t, n_peers)),
                dst_ref=target_at,
                send_sem=send.at[d * n_peers + t],
                recv_sem=recv.at[d * n_peers + t],
                device_id=dict(near_id(t), dom=lax.rem(dom + d, n_dom)),
                device_id_type=MESH,
            )
            for d, t in others
        ]

    barrier = pltpu.get_barrier_semaphore()
    for d in range(n_dom):
        for t in range(n_peers):
            if d or t:
                pl.semaphore_signal(
                    barrier,
                    inc=1,
                    device_id=dict(near_id(t), dom=lax.rem(dom + d, n_dom)),
                    device_id_type=MESH,
                )

    lane = lax.broadcasted_iota(jnp.int32, (1, LANES), 1)

    for copy in copies[:5]:
        copy.wait()

    for c in range(3):
        tab[c, owned:, :] = jnp.zeros((LANES - owned, LANES), F32)
        for h in range(owned):
            tab[c, h : h + 1, :] = disp[c : c + 1, h * LANES : (h + 1) * LANES]

    def turn(source, table):
        for c in range(3):
            top, rest = split(source[c].T)
            table[c * LANES : (c + 1) * LANES, :LANES] = top
            table[c * LANES : (c + 1) * LANES, LANES:] = rest

    turn(tab, table)

    far_index[...] = jnp.zeros_like(far_index)
    far_index[:n_dom, :64] = far_lists[...]
    listed = far_index[...]
    lane_f = lax.broadcasted_iota(jnp.int32, listed.shape, 1)
    listed = jnp.where(lane_f < 64, listed, pltpu.roll(listed, 64, 1))
    far_rows = [
        jnp.where((lane & 63) < far_counts[p], listed[p : p + 1], NOWHERE) for p in range(n_dom)
    ]
    near_rows = [
        jnp.where(lane < near_counts[t], near_lists[t : t + 1, :], NOWHERE)
        for t in range(n_peers)
    ]

    own_rows = [jnp.where(row < node_count, row, NOWHERE) for row in near_rows]
    far_keys = [
        jnp.where(
            (row >= node_count) & (row < NOWHERE),
            row + (peer * (n_dom * CAP_FAR) - node_count),
            NOWHERE,
        )
        for row in near_rows
    ]

    far_out[...] = jnp.zeros_like(far_out)
    near_out[...] = jnp.zeros_like(near_out)
    ghost_out[...] = jnp.zeros_like(ghost_out)
    back_out[...] = jnp.zeros_like(back_out)

    found = pick(table[...], far_rows + own_rows)
    for p in range(n_dom):
        for c in range(3):
            far_out[p, c : c + 1, :] = found[c][p]
    for t in range(n_peers):
        for c in range(3):
            near_out[t, c : c + 1, :] = found[c][n_dom + t]
        near_out[t, 3:4, :] = far_keys[t].astype(F32)
    for s in range(n_peers):
        far_in[s, dom] = jnp.zeros((8, LANES), F32)
        back_in[dom, s] = jnp.zeros((8, LANES), F32)

    pl.semaphore_wait(barrier, n_dom * n_peers - 1)
    far_sends = far_copies(
        lambda d, t: far_out.at[lax.rem(dom + d, n_dom)],
        far_in.at[peer, dom],
        send_far,
        recv_far,
    )
    near_sends = near_copies(near_out, near_in, send_near, recv_near)
    for copy in far_sends + near_sends:
        copy.start()
    near_in[peer] = near_out[peer]

    for copy in copies[5:]:
        copy.wait()

    tab_rows = jnp.full((8, LANES), NOWHERE, jnp.int32)
    index[0, 120:128, :] = tab_rows
    index[0, :125, :] = conn[...]
    low_half = index[0, :ROWS, :]
    high_half = index[0, ROWS:, :]
    lane64 = lax.broadcasted_iota(jnp.int32, (ROWS, LANES), 1)
    packed_in = jnp.where(lane64 < 64, low_half, pltpu.roll(high_half, 64, 1))
    packed_out = jnp.where(lane64 < 64, pltpu.roll(low_half, 64, 1), high_half)
    index[1, :ROWS, :] = packed_in
    index[1, ROWS:, :] = packed_out

    first[120:128, :] = jnp.zeros((8, LANES), F32)
    shear[120:128, :] = jnp.zeros((8, LANES), F32)
    first[:125, :] = lame_first[...].astype(F32)
    shear[:125, :] = lame_shear[...].astype(F32)

    def gather(half):
        def body(step, _):
            at = pl.multiple_of(half * ROWS + step * 8, 8)
            block = index[1, pl.ds(at, 8), :]
            got = pick(table[...], [block[r : r + 1] for r in range(8)])
            for c in range(3):
                nodal[c, pl.ds(at, 8), :] = jnp.concatenate(got[c], axis=0)
            return 0

        lax.fori_loop(0, ROWS // 8, body, 0)

    def scatter(half, acc):
        acc[...] = jnp.zeros_like(acc)

        def body(step, _):
            at = pl.multiple_of(half * ROWS + step * 8, 8)
            block = index[1, pl.ds(at, 8), :]
            terms = [nodal[c, pl.ds(at, 8), :] for c in range(3)]
            acc[...] += spread(
                [block[r : r + 1] for r in range(8)],
                [[terms[c][r : r + 1] for r in range(8)] for c in range(3)],
            )
            return 0

        lax.fori_loop(0, ROWS // 8, body, 0)

    def elements(half):
        rows = slice(half * ROWS, (half + 1) * ROWS)
        columns = []
        for c in range(3):
            packed = nodal[c, rows, :]
            turned = pltpu.roll(packed, 64, 1)
            columns.append(jnp.concatenate([packed, turned], axis=0))
        top, rest = split(jnp.concatenate(columns, axis=1))
        gref = jnp.dot(
            fwd[...], jnp.concatenate([top, top, rest], axis=0), preferred_element_type=F32
        )
        jacobian = jac[...]
        lam = first[...]
        mu = shear[...]
        if half == 1:
            jacobian = pltpu.roll(jacobian, 64, 1)
            lam = pltpu.roll(lam, 64, 1)
            mu = pltpu.roll(mu, 64, 1)
        factor = [[jacobian[3 * r + i : 3 * r + i + 1] for i in range(3)] for r in range(3)]
        ref = [
            [
                gref[r * LANES : (r + 1) * LANES, c * LANES : (c + 1) * LANES]
                for r in range(3)
            ]
            for c in range(3)
        ]
        grad = [
            [
                factor[0][i] * ref[c][0] + factor[1][i] * ref[c][1] + factor[2][i] * ref[c][2]
                for i in range(3)
            ]
            for c in range(3)
        ]
        trace = lam * (grad[0][0] + grad[1][1] + grad[2][2])
        stress = [[None] * 3 for _ in range(3)]
        for c in range(3):
            stress[c][c] = 2.0 * mu * grad[c][c] + trace
            for i in range(c + 1, 3):
                stress[c][i] = stress[i][c] = mu * (grad[c][i] + grad[i][c])
        tref = jnp.concatenate(
            [
                jnp.concatenate(
                    [
                        factor[r][0] * stress[c][0]
                        + factor[r][1] * stress[c][1]
                        + factor[r][2] * stress[c][2]
                        for c in range(3)
                    ],
                    axis=1,
                )
                for r in range(3)
            ],
            axis=0,
        )
        top, rest = split(tref)
        result = jnp.dot(
            bwd[...], jnp.concatenate([top, top, rest], axis=0), preferred_element_type=F32
        )
        for c in range(3):
            part = result[:, c * LANES : (c + 1) * LANES]
            nodal[c, rows, :] = jnp.where(
                lane64 < 64, part[:ROWS], pltpu.roll(part[ROWS:], 64, 1)
            )

    gather(0)

    elements(0)

    far_tab[...] = jnp.zeros_like(far_tab)
    for copy in far_sends + near_sends:
        copy.wait()
    for s in range(n_peers):
        for j in range(far_rows_each):
            at = s * far_rows_each + j
            for c in range(3):
                far_tab[c, at : at + 1, :] = jnp.where(
                    lane < 64, far_in[s, 2 * j, c : c + 1, :], far_in[s, 2 * j + 1, c : c + 1, :]
                )
    turn(far_tab, far_table)
    ghost_keys = [near_in[s, 3:4, :].astype(jnp.int32) for s in range(n_peers)]
    found = pick(far_table[...], ghost_keys)
    for c in range(3):
        for s in range(n_peers):
            tab[c, owned + s : owned + s + 1, :] = near_in[s, c : c + 1, :] + found[c][s]
    turn(tab, table)
    gather(1)
    elements(1)
    scatter(1, acc_out)
    outer = acc_out[...]
    kept = owned // 2
    for c in range(3):
        whole = joined(outer, c)
        for s in range(n_peers):
            half = (s % 2) * LANES
            ghost_out[s, c : c + 1, :] = whole[kept + s // 2 : kept + s // 2 + 1, half : half + LANES]
    far_height = -(-n_peers * n_dom * CAP_FAR // (2 * LANES) // 16) * 16
    beyond = spread(
        ghost_keys,
        [[ghost_out[s, c : c + 1, :] for s in range(n_peers)] for c in range(3)],
        far_height,
    )
    for c in range(3):
        whole = joined(beyond, c, far_height)
        for s in range(n_peers):
            for p in range(n_dom):
                row = s * (far_rows_each // 2) + p // 4
                half = ((p // 2) % 2) * LANES
                back_out[p, s, c : c + 1, :] = whole[row : row + 1, half : half + LANES]
    sends = near_copies(ghost_out, ghost_in, send_ghost, recv_ghost) + far_copies(
        lambda d, t: back_out.at[lax.rem(dom + d, n_dom), t],
        back_in.at[dom, peer],
        send_back,
        recv_back,
    )
    for copy in sends:
        copy.start()
    ghost_in[peer] = ghost_out[peer]

    scatter(0, acc_in)
    mine = (lane >> 6) == lax.rem(dom, 2)
    back_rows = [jnp.where(mine, far_rows[p], NOWHERE) for p in range(n_dom)]

    for copy in sends:
        copy.wait()
    arrived = [back_in[p, 0] for p in range(n_dom)]
    for t in range(1, n_peers):
        arrived = [arrived[p] + back_in[p, t] for p in range(n_dom)]
    total = acc_in[...] + acc_out[...]
    total = total + spread(
        own_rows + back_rows,
        [
            [ghost_in[t, c : c + 1, :] for t in range(n_peers)]
            + [arrived[p][c : c + 1, :] for p in range(n_dom)]
            for c in range(3)
        ],
    )
    for c in range(3):
        whole = joined(total, c)
        for q in range(kept):
            out[c : c + 1, q * 2 * LANES : (q + 1) * 2 * LANES] = whole[q : q + 1]


def local(
    n_dom,
    n_sub,
    n_comp,
    displacement,
    far_lists,
    far_counts,
    near_lists,
    near_counts,
    connectivity,
    inverse_jacobian,
    lame_first,
    lame_shear,
):
    n_peers = n_sub * n_comp
    fwd, bwd = split_tables()
    operands = (
        far_counts,
        near_counts,
        displacement,
        far_lists,
        near_lists,
        connectivity,
        inverse_jacobian,
        lame_first,
        lame_shear,
        jnp.asarray(fwd),
        jnp.asarray(bwd),
    )
    near_slots = pltpu.VMEM((n_peers, 8, LANES), F32)
    return pl.pallas_call(
        functools.partial(kernel, n_dom, n_sub, n_comp),
        out_shape=jax.ShapeDtypeStruct(displacement.shape, F32),
        in_specs=[pl.BlockSpec(memory_space=pltpu.HBM)] * 11,
        out_specs=pl.BlockSpec(memory_space=pltpu.VMEM),
        scratch_shapes=[
            pltpu.SMEM(operands[0].shape, jnp.int32),
            pltpu.SMEM(operands[1].shape, jnp.int32),
        ]
        + [pltpu.VMEM(x.shape, x.dtype) for x in operands[2:]]
        + [
            pltpu.VMEM((3, LANES, LANES), F32),
            pltpu.VMEM((3 * LANES, 2 * LANES), BF16),
            pltpu.VMEM((3, LANES, LANES), F32),
            pltpu.VMEM((3 * LANES, 2 * LANES), BF16),
            pltpu.VMEM((max(8, n_dom), LANES), jnp.int32),
            pltpu.VMEM((2, 2 * ROWS, LANES), jnp.int32),
            pltpu.VMEM((3, 2 * ROWS, LANES), F32),
            pltpu.VMEM((LANES, LANES), F32),
            pltpu.VMEM((LANES, LANES), F32),
            pltpu.VMEM((6 * HIGH, 2 * LANES), F32),
            pltpu.VMEM((6 * HIGH, 2 * LANES), F32),
            pltpu.VMEM((n_dom, 8, LANES), F32),
            pltpu.VMEM((n_peers, n_dom, 8, LANES), F32),
            near_slots,
            near_slots,
            near_slots,
            near_slots,
            pltpu.VMEM((n_dom, n_peers, 8, LANES), F32),
            pltpu.VMEM((n_dom, n_peers, 8, LANES), F32),
        ]
        + [pltpu.SemaphoreType.DMA((n_dom * n_peers,))] * 2
        + [pltpu.SemaphoreType.DMA((n_peers,))] * 4
        + [pltpu.SemaphoreType.DMA((n_dom * n_peers,))] * 2
        + [pltpu.SemaphoreType.DMA((11,))],
        compiler_params=pltpu.CompilerParams(
            collective_id=0, has_side_effects=True
        ),
    )(*operands)


def solution(mesh):
    spread_axes = ("groups", "dom", "sub", "comp")
    rows = P(spread_axes, None)
    columns = P(None, spread_axes)
    flat = P(spread_axes)
    in_specs = (columns, rows, flat, rows, flat, columns, columns, columns, columns)
    sizes = (mesh.shape["dom"], mesh.shape["sub"], mesh.shape["comp"])
    return jax.shard_map(
        functools.partial(local, *sizes),
        mesh=mesh,
        in_specs=in_specs,
        out_specs=columns,
        check_vma=False,
    )
```
